768 devices in a mesh: blk: 96 (over x, z, y_hi), rep: 8 (over y_lo, core).
Axes of the slice: x: 4, y: 8 (y_hi: 2, y_lo: 4; y = y_hi * 4 + y_lo), z: 12, core: 2. Of those that a mesh axis runs over, the one named last changes fastest.
Arguments:
- features: bfloat16 [786432, 128], P(('blk', 'rep')), may hold values from -6 to 6
- neighbours: int32 [786432, 10], P(('blk', 'rep')), may hold values from 0 to 5119
- w_self: bfloat16 [128, 512], replicated, may hold values from -0.5 to 0.5
- w_neigh: bfloat16 [128, 512], replicated, may hold values from -0.5 to 0.5
- bias: float32 [512], replicated, may hold values from -4 to 4
- cotangent: bfloat16 [786432, 512], P(('blk', 'rep')), may hold values from -6 to 6
Outputs:
- hidden: bfloat16 [786432, 512], P(('blk', 'rep'))
- grad_x: bfloat16 [786432, 128], P(('blk', 'rep'))
- grad_self: float32 [128, 512], replicated
- grad_neigh: float32 [128, 512], replicated
- grad_bias: float32 [512], replicated
The draws below stay inside these ranges and needn't reach their ends.
Inputs may be any that keep to these rules, and one draw needn't show every extreme that they name: `neighbours`: A value v refers to loop position 4 or fewer steps back: v // 1024 steps.
All inputs are finite; a program needn't handle non-finite values.
Results may differ from the reference program's by a relative error of at most 0.007.
Values may be sent and summed in bfloat16 or wider, within the bound.
No kernel may reach another device: no remote copies, remote signals or barrier semaphores. Data moves between devices by JAX's collectives and lax.ppermute only.
A program may use at most 32 MiB of HBM per device.

```python
import jax
import jax.numpy as jnp
from jax import lax

FIN = 128
HID = 512
FAN = 10
STEPS = 4
ROWS = 1024
NODES = 786432
N_BLK = 96
N_REP = 8


def place_ends(entries, own_key, least, high):
    shape = entries.shape
    place = [jax.random.randint(jax.random.fold_in(own_key, axis), (), 0, shape[axis]) for axis in range(len(shape))]
    entries = entries.at[tuple(place)].set(least)
    longest = shape.index(max(shape))
    place[longest] = (place[longest] + 1) % shape[longest]
    return entries.at[tuple(place)].set(high)


def block_scale(own_key, extent, split, low, high):
    def one(axis_at, blocks):
        draws = jax.random.uniform(jax.random.fold_in(jax.random.fold_in(own_key, 6), axis_at), (blocks,), jnp.float32, low / len(split), high / len(split))
        return jnp.repeat(jnp.exp(draws), extent[axis_at] // blocks).reshape((-1,) + (1,) * (len(extent) - axis_at - 1))

    level = one(*split[0])
    for cut in split[1:]:
        level = level * one(*cut)
    return level


def bell_draw(own_key, shape, scale, bound, split=(), held_as=jnp.bfloat16):
    factor_of = block_scale(own_key, shape, split, -0.22, 0.18) if split else 1.0
    drawn = jax.random.normal(own_key, shape, jnp.float32) * scale * factor_of
    return jnp.minimum(jnp.maximum(drawn, -bound), bound).astype(held_as)


def setup_inputs(seed: int = 0) -> dict:
    seeds = jax.random.split(jax.random.key(seed), 7)
    return {
        "features": bell_draw(seeds[0], (NODES, FIN), 1.0, 6.0, ((0, 768),)),
        "neighbours": place_ends(jax.random.randint(seeds[1], (NODES, FAN), 0, (STEPS + 1) * ROWS), jax.random.fold_in(seeds[1], 1), 0, ((STEPS + 1) * ROWS) - 1).astype(jnp.int32),
        "w_self": bell_draw(seeds[2], (FIN, HID), FIN ** -0.5, 0.5),
        "w_neigh": bell_draw(seeds[3], (FIN, HID), FIN ** -0.5, 0.5),
        "bias": bell_draw(seeds[4], (HID,), 1.0, 4.0, (), jnp.float32),
        "cotangent": bell_draw(seeds[5], (NODES, HID), 1.0, 6.0, ((0, 768),)),
    }


def reference(features, neighbours, w_self, w_neigh, bias, cotangent):
    nodes = features.shape[0]
    blocks = nodes // ROWS
    scale = 1.0 / (nodes ** 0.5)

    def source_rows(block):
        near = lax.dynamic_slice_in_dim(neighbours, block * ROWS, ROWS, 0)
        back = near // ROWS
        local = near % ROWS
        anchor = ((block // N_REP - back) % N_BLK) * N_REP + block % N_REP
        return (anchor * ROWS + local).astype(jnp.int32)

    def step_block(carry, block):
        accum, g_self, g_neigh, g_bias = carry
        src = source_rows(block)
        start = (block * ROWS).astype(jnp.int32)
        own = lax.dynamic_slice_in_dim(features, start, ROWS, 0)
        tangent = lax.dynamic_slice_in_dim(cotangent, start, ROWS, 0)
        gathered = features[src].astype(jnp.float32)
        mean = (jnp.sum(gathered, axis=1) / FAN).astype(jnp.bfloat16)
        pre = jnp.dot(own, w_self, preferred_element_type=jnp.float32) + jnp.dot(mean, w_neigh, preferred_element_type=jnp.float32) + bias
        sig = jax.nn.sigmoid(pre)
        hidden = (pre * sig).astype(jnp.bfloat16)
        dpre = (tangent.astype(jnp.float32) * sig * (1.0 + pre * (1.0 - sig))).astype(jnp.bfloat16)
        g_self = g_self + jnp.dot(own.T, dpre, preferred_element_type=jnp.float32)
        g_neigh = g_neigh + jnp.dot(mean.T, dpre, preferred_element_type=jnp.float32)
        g_bias = g_bias + jnp.sum(dpre.astype(jnp.float32), axis=0)
        dself = jnp.dot(dpre, w_self.T, preferred_element_type=jnp.float32)
        dmean = (jnp.dot(dpre, w_neigh.T, preferred_element_type=jnp.float32) / FAN).astype(jnp.bfloat16)
        own_rows = start + jnp.arange(ROWS, dtype=jnp.int32)
        accum = accum.at[own_rows].add(dself)
        spread = jnp.broadcast_to(dmean.astype(jnp.float32)[:, None, :], (ROWS, FAN, FIN)).reshape(ROWS * FAN, FIN)
        accum = accum.at[src.reshape(-1)].add(spread)
        return (accum, g_self, g_neigh, g_bias), hidden

    init = (jnp.zeros((nodes, FIN), jnp.float32), jnp.zeros((FIN, HID), jnp.float32), jnp.zeros((FIN, HID), jnp.float32), jnp.zeros((HID,), jnp.float32))
    final, hidden = lax.scan(step_block, init, jnp.arange(blocks, dtype=jnp.int32))
    accum, g_self, g_neigh, g_bias = final
    return hidden.reshape(nodes, HID), accum.astype(jnp.bfloat16), g_self * scale, g_neigh * scale, g_bias * scale
```

```python
import functools

import jax
import jax.numpy as jnp
import numpy as np
from jax import lax
from jax.experimental import pallas as pl
from jax.experimental.pallas import tpu as pltpu
from jax.sharding import Mesh
from jax.sharding import PartitionSpec as P

FAN = 10
STEPS = 4
WINDOW_TILE = 256
NODE_TILE = 256
LANES = 128
SUBLANES = 8
PACK = 16
VMEM = 24 * 1024 * 1024
BF16 = jnp.bfloat16
F32 = jnp.float32

GRID = (("x", 4), ("z", 12), ("far", 2), ("near", 4), ("core", 2))
AXES = tuple(name for name, _ in GRID)
FIRST = ("x", "far", "near", "core")
SECOND = ("z",)

ROWS_FIRST = (((0,), (0,)), ((), ()))
COLS_LAST = (((1,), (1,)), ((), ()))


def dot(a, b, contract=(((1,), (0,)), ((), ()))):
    return lax.dot_general(a, b, contract, preferred_element_type=F32)


def count_kernel(near_ref, out_ref):
    row = lax.broadcasted_iota(jnp.int32, (PACK, LANES), 0)
    rows = [(row + PACK * g).astype(jnp.int16) for g in range(WINDOW_TILE // PACK)]
    one = jnp.ones((PACK, LANES), BF16)
    zero = jnp.zeros((PACK, LANES), BF16)

    @pl.loop(0, out_ref.shape[0] // WINDOW_TILE)
    def _(step):
        low = pl.multiple_of(step * WINDOW_TILE, WINDOW_TILE)
        key = (near_ref[...] - low).astype(jnp.int16)
        for lane in range(near_ref.shape[1] // LANES):
            cols = slice(lane * LANES, (lane + 1) * LANES)
            keys = [jnp.broadcast_to(key[k : k + 1, cols], (PACK, LANES)) for k in range(FAN)]
            for g in range(WINDOW_TILE // PACK):
                count = jnp.where(rows[g] == keys[0], one, zero)
                for k in range(1, FAN):
                    count = count + jnp.where(rows[g] == keys[k], one, zero)
                out_ref[pl.ds(low + g * PACK, PACK), cols] = count


def in_vmem():
    return pl.BlockSpec(memory_space=pltpu.VMEM)


def count_tiles(near):
    entries, rows = near.shape
    window = (STEPS + 1) * rows
    return pl.pallas_call(
        count_kernel,
        in_specs=[in_vmem()],
        out_specs=in_vmem(),
        out_shape=jax.ShapeDtypeStruct((window, rows), BF16),
        cost_estimate=pl.CostEstimate(
            flops=3 * entries * window * rows, bytes_accessed=2 * window * rows, transcendentals=0
        ),
        compiler_params=pltpu.CompilerParams(vmem_limit_bytes=VMEM),
        name="count_tiles",
    )(near)


def whole(array):
    return pl.BlockSpec(array.shape, lambda *_: (0,) * array.ndim)


def gather_kernel(window_blocks, tile_ref, *refs):
    *blocks, out_ref = refs
    rows = blocks[0].shape[0]
    total = None
    for back, block in zip(window_blocks, blocks):
        term = dot(block[...], tile_ref[back * rows : (back + 1) * rows, :], ROWS_FIRST)
        total = term if total is None else total + term
    out_ref[...] = total


def gather_sum(tiles, window_blocks, blocks):
    rows, width = blocks[0].shape
    steps = len(blocks)
    return pl.pallas_call(
        functools.partial(gather_kernel, window_blocks),
        in_specs=[in_vmem()] * (1 + steps),
        out_specs=in_vmem(),
        out_shape=jax.ShapeDtypeStruct((width, rows), F32),
        cost_estimate=pl.CostEstimate(
            flops=2 * steps * rows * rows * width,
            bytes_accessed=2 * steps * rows * width,
            transcendentals=0,
        ),
        compiler_params=pltpu.CompilerParams(vmem_limit_bytes=VMEM),
        name="gather_sum",
    )(tiles, *blocks)


def layer_kernel(
    back,
    chunk_rows,
    tile_ref,
    part_ref,
    block_ref,
    w_self_ref,
    w_neigh_ref,
    bias_ref,
    own_ref,
    cot_ref,
    hidden_ref,
    send_ref,
    own_part_ref,
    near_part_ref,
    far_part_ref,
    total_ref,
    grad_ref,
    gbias_ref,
    w_ref,
    dmean_ref,
):
    rows, width = block_ref.shape
    hid = w_ref.shape[1]
    step = pl.program_id(0)

    @pl.when(step == 0)
    def _():
        tile = tile_ref[back * rows : (back + 1) * rows, :]
        total_ref[...] = part_ref[...] + dot(block_ref[...], tile, ROWS_FIRST)
        grad_ref[...] = jnp.zeros_like(grad_ref)
        gbias_ref[...] = jnp.zeros_like(gbias_ref)
        w_ref[:width, :] = w_self_ref[...]
        w_ref[width:, :] = w_neigh_ref[...]

    weights = w_ref[...]
    span = pl.ds(pl.multiple_of(step * NODE_TILE, NODE_TILE), NODE_TILE)
    mean = (total_ref[:, span].T / FAN).astype(BF16)
    both = jnp.concatenate([own_ref[...], mean], axis=1)
    pre = dot(both, weights) + bias_ref[...]
    sig = jax.nn.sigmoid(pre)
    hidden_ref[...] = (pre * sig).astype(BF16)
    slope = sig * (1.0 + pre * (1.0 - sig))
    dpre = (cot_ref[...].astype(F32) * slope).astype(BF16)
    grad_ref[...] += dot(both, dpre, ROWS_FIRST)
    gbias_ref[...] += jnp.sum(dpre.astype(F32), axis=0, keepdims=True)
    back_both = dot(dpre, weights, COLS_LAST)
    own_part_ref[span, :] = back_both[:, :width]
    dmean_ref[span, :] = (back_both[:, width:] / FAN).astype(BF16)

    @pl.when(step == pl.num_programs(0) - 1)
    def _():
        pieces = hid // LANES
        spare = send_ref.shape[1] - chunk_rows - pieces
        folded = [gbias_ref[:, p * LANES : (p + 1) * LANES] for p in range(pieces)]
        folded = jnp.concatenate([*folded, jnp.zeros((spare, LANES), F32)], axis=0)
        for chunk in range(send_ref.shape[0]):
            top, left = chunk // pieces * chunk_rows, chunk % pieces * LANES
            term = grad_ref[top : top + chunk_rows, left : left + LANES]
            send_ref[chunk] = jnp.concatenate([term, folded], axis=0).astype(BF16)
        dmean = dmean_ref[...]
        for steps_back in reversed(range(STEPS + 1)):
            term = dot(tile_ref[steps_back * rows : (steps_back + 1) * rows, :], dmean)
            if steps_back == 0:
                own_part_ref[...] += term
            else:
                out_ref, at = (near_part_ref, 1) if steps_back < 3 else (far_part_ref, 3)
                first = (steps_back - at) * rows
                out_ref[first : first + rows, :] = term.astype(BF16)


def layer(tiles, part, block, back, own, w_self, w_neigh, bias, cotangent, copies):
    rows, width = own.shape
    hid = w_self.shape[1]
    chunk_rows = 2 * width * hid // (copies * LANES)
    bias_rows = -(-hid // (LANES * SUBLANES)) * SUBLANES

    def tiled(columns):
        return pl.BlockSpec((NODE_TILE, columns), lambda i: (i, 0))

    outs = (
        jax.ShapeDtypeStruct((rows, hid), BF16),
        jax.ShapeDtypeStruct((copies, chunk_rows + bias_rows, LANES), BF16),
        jax.ShapeDtypeStruct((rows, width), F32),
        jax.ShapeDtypeStruct((2 * rows, width), BF16),
        jax.ShapeDtypeStruct((2 * rows, width), BF16),
    )
    return pl.pallas_call(
        functools.partial(layer_kernel, back, chunk_rows),
        grid=(rows // NODE_TILE,),
        in_specs=[in_vmem()] * 6 + [tiled(width), tiled(hid)],
        out_specs=[tiled(hid)] + [whole(o) for o in outs[1:]],
        out_shape=outs,
        scratch_shapes=[
            pltpu.VMEM((width, rows), F32),
            pltpu.VMEM((2 * width, hid), F32),
            pltpu.VMEM((1, hid), F32),
            pltpu.VMEM((2 * width, hid), BF16),
            pltpu.VMEM((rows, width), BF16),
        ],
        cost_estimate=pl.CostEstimate(
            flops=12 * rows * rows * width + 12 * rows * width * hid,
            bytes_accessed=4 * rows * hid,
            transcendentals=2 * rows * hid,
        ),
        compiler_params=pltpu.CompilerParams(vmem_limit_bytes=VMEM),
        name="layer",
    )(tiles, part, block, w_self, w_neigh, bias, own, cotangent)


def unfold_kernel(chunks_ref, *out_refs):
    rows, columns = out_refs[0].shape
    copies, chunk_rows, lanes = chunks_ref.shape
    pieces = columns // lanes
    for chunk in range(copies):
        top, left = chunk // pieces * chunk_rows, chunk % pieces * lanes
        out_ref, top = out_refs[top // rows], top % rows
        out_ref[top : top + chunk_rows, left : left + lanes] = chunks_ref[chunk].astype(F32)


def unfold(chunks, rows, columns):
    return pl.pallas_call(
        unfold_kernel,
        out_shape=[jax.ShapeDtypeStruct((rows, columns), F32)] * 2,
        compiler_params=pltpu.CompilerParams(vmem_limit_bytes=VMEM),
        name="unfold",
    )(chunks)


def shift_pairs(by):
    sizes = [n for _, n in GRID]
    group = sizes[3] * sizes[4]
    peers = sizes[0] * sizes[1] * sizes[2]
    return [
        (b * group + r, ((b + by) % peers) * group + r) for b in range(peers) for r in range(group)
    ]


def shifted(array, by):
    return lax.ppermute(array, AXES, shift_pairs(by))


def exchange(array, axes):
    return lax.all_to_all(array, axes, 0, 0, tiled=True)


def sum_parts(array):
    return jnp.sum(array.astype(F32), axis=0)


def to_all(array, axes):
    return exchange(jnp.broadcast_to(array[None], (lax.axis_size(axes),) + array.shape), axes)


def shards(features, neighbours, w_self, w_neigh, bias, cotangent):
    rows, width = features.shape
    hid = w_self.shape[1]
    n_first = lax.axis_size(FIRST)
    near1 = shifted(features, 1)
    near2 = shifted(features, 2)
    near4 = shifted(features, 4)
    tiles = count_tiles(neighbours.T)
    near1, tiles = lax.optimization_barrier((near1, tiles))
    near3 = shifted(near1, 2)
    part = gather_sum(tiles, (0, 2, 4, 1), (features, near2, near4, near1))
    hidden, send, own, near, far = layer(
        tiles, part, near3, 3, features, w_self, w_neigh, bias[None], cotangent, n_first
    )
    far = shifted(far, -2)
    chunk = sum_parts(exchange(send, FIRST)).astype(BF16)
    far, _ = lax.optimization_barrier((far, chunk))
    near = near.astype(F32) + far.astype(F32)
    got1 = shifted(near[:rows].astype(BF16), -1)
    got2 = shifted(near[rows:].astype(BF16), -2)

    scale = 1.0 / (rows * lax.axis_size(AXES)) ** 0.5
    total = sum_parts(to_all(chunk, SECOND)) * scale
    pieces = hid // LANES
    chunk_rows = 2 * width * pieces // n_first
    grads = unfold(to_all(total[:chunk_rows].astype(BF16), FIRST), width, hid)
    g_bias = total[chunk_rows : chunk_rows + pieces].reshape(hid)
    grad_x = own + got1.astype(F32) + got2.astype(F32)
    return hidden, grad_x.astype(BF16), *grads, g_bias


def solution(mesh):
    grid = Mesh(mesh.devices.reshape([n for _, n in GRID]), AXES)
    node = P(AXES, None)
    return jax.shard_map(
        shards,
        mesh=grid,
        in_specs=(node, node, P(), P(), P(), node),
        out_specs=(node, node, P(), P(), P()),
        check_vma=False,
    )
```

```python
import functools

import jax
import jax.numpy as jnp
import numpy as np
from jax import lax
from jax.experimental import pallas as pl
from jax.experimental.pallas import tpu as pltpu
from jax.sharding import Mesh
from jax.sharding import PartitionSpec as P

FAN = 10
STEPS = 4
CLOSE = 3
WINDOW_TILE = 256
NODE_TILE = 256
LANES = 128
SUBLANES = 8
PACK = 16
VMEM = 24 * 1024 * 1024
BF16 = jnp.bfloat16
F32 = jnp.float32

GRID = (("x", 4), ("z", 12), ("far", 2), ("near", 4), ("core", 2))
AXES = tuple(name for name, _ in GRID)
FIRST = ("x", "far", "near", "core")
SECOND = ("z",)

ROWS_FIRST = (((0,), (0,)), ((), ()))
COLS_LAST = (((1,), (1,)), ((), ()))


def dot(a, b, contract=(((1,), (0,)), ((), ()))):
    return lax.dot_general(a, b, contract, preferred_element_type=F32)


def count_kernel(first, near_ref, out_ref):
    row = lax.broadcasted_iota(jnp.int32, (PACK, LANES), 0)
    rows = [(row + PACK * g).astype(jnp.int16) for g in range(WINDOW_TILE // PACK)]
    one = jnp.ones((PACK, LANES), BF16)
    zero = jnp.zeros((PACK, LANES), BF16)

    @pl.loop(0, out_ref.shape[0] // WINDOW_TILE)
    def _(step):
        low = pl.multiple_of(step * WINDOW_TILE, WINDOW_TILE)
        key = (near_ref[...] - (first + low)).astype(jnp.int16)
        for lane in range(near_ref.shape[1] // LANES):
            cols = slice(lane * LANES, (lane + 1) * LANES)
            keys = [jnp.broadcast_to(key[k : k + 1, cols], (PACK, LANES)) for k in range(FAN)]
            for g in range(WINDOW_TILE // PACK):
                count = jnp.where(rows[g] == keys[0], one, zero)
                for k in range(1, FAN):
                    count = count + jnp.where(rows[g] == keys[k], one, zero)
                out_ref[pl.ds(low + g * PACK, PACK), cols] = count


def in_vmem():
    return pl.BlockSpec(memory_space=pltpu.VMEM)


def count_tiles(near, first, blocks):
    entries, rows = near.shape
    window = blocks * rows
    return pl.pallas_call(
        functools.partial(count_kernel, first * rows),
        in_specs=[in_vmem()],
        out_specs=in_vmem(),
        out_shape=jax.ShapeDtypeStruct((window, rows), BF16),
        cost_estimate=pl.CostEstimate(
            flops=3 * entries * window * rows, bytes_accessed=2 * window * rows, transcendentals=0
        ),
        compiler_params=pltpu.CompilerParams(vmem_limit_bytes=VMEM),
        name="count_tiles",
    )(near)


def whole(array):
    return pl.BlockSpec(array.shape, lambda *_: (0,) * array.ndim)


def tile_of(back, close_ref, far_ref):
    rows = close_ref.shape[1]
    ref, first = (close_ref, 0) if back < CLOSE else (far_ref, CLOSE)
    return ref[(back - first) * rows : (back - first + 1) * rows, :]


def gather_kernel(window_blocks, close_ref, far_ref, *refs):
    *blocks, out_ref = refs
    total = None
    for back, block in zip(window_blocks, blocks):
        term = dot(block[...], tile_of(back, close_ref, far_ref), ROWS_FIRST)
        total = term if total is None else total + term
    out_ref[...] = total


def gather_sum(tiles, window_blocks, blocks):
    rows, width = blocks[0].shape
    steps = len(blocks)
    return pl.pallas_call(
        functools.partial(gather_kernel, window_blocks),
        in_specs=[in_vmem()] * (2 + steps),
        out_specs=in_vmem(),
        out_shape=jax.ShapeDtypeStruct((width, rows), F32),
        cost_estimate=pl.CostEstimate(
            flops=2 * steps * rows * rows * width,
            bytes_accessed=2 * steps * rows * width,
            transcendentals=0,
        ),
        compiler_params=pltpu.CompilerParams(vmem_limit_bytes=VMEM),
        name="gather_sum",
    )(*tiles, *blocks)


def layer_kernel(
    back,
    chunk_rows,
    close_ref,
    far_ref,
    part_ref,
    block_ref,
    w_self_ref,
    w_neigh_ref,
    bias_ref,
    own_ref,
    cot_ref,
    hidden_ref,
    send_ref,
    dself_ref,
    dmean_ref,
    far_part_ref,
    total_ref,
    grad_ref,
    gbias_ref,
    w_ref,
):
    rows, width = block_ref.shape
    hid = w_ref.shape[1]
    step = pl.program_id(0)

    @pl.when(step == 0)
    def _():
        tile = tile_of(back, close_ref, far_ref)
        total_ref[...] = part_ref[...] + dot(block_ref[...], tile, ROWS_FIRST)
        grad_ref[...] = jnp.zeros_like(grad_ref)
        gbias_ref[...] = jnp.zeros_like(gbias_ref)
        w_ref[:width, :] = w_self_ref[...]
        w_ref[width:, :] = w_neigh_ref[...]

    weights = w_ref[...]
    span = pl.ds(pl.multiple_of(step * NODE_TILE, NODE_TILE), NODE_TILE)
    mean = (total_ref[:, span].T / FAN).astype(BF16)
    both = jnp.concatenate([own_ref[...], mean], axis=1)
    pre = dot(both, weights) + bias_ref[...]
    sig = jax.nn.sigmoid(pre)
    hidden_ref[...] = (pre * sig).astype(BF16)
    slope = sig * (1.0 + pre * (1.0 - sig))
    dpre = (cot_ref[...].astype(F32) * slope).astype(BF16)
    grad_ref[...] += dot(both, dpre, ROWS_FIRST)
    gbias_ref[...] += jnp.sum(dpre.astype(F32), axis=0, keepdims=True)
    back_both = dot(dpre, weights, COLS_LAST)
    dself_ref[span, :] = back_both[:, :width]
    dmean_ref[span, :] = (back_both[:, width:] / FAN).astype(BF16)

    @pl.when(step == pl.num_programs(0) - 1)
    def _():
        pieces = hid // LANES
        spare = send_ref.shape[1] - chunk_rows - pieces
        folded = [gbias_ref[:, p * LANES : (p + 1) * LANES] for p in range(pieces)]
        folded = jnp.concatenate([*folded, jnp.zeros((spare, LANES), F32)], axis=0)
        for chunk in range(send_ref.shape[0]):
            top, left = chunk // pieces * chunk_rows, chunk % pieces * LANES
            term = grad_ref[top : top + chunk_rows, left : left + LANES]
            send_ref[chunk] = jnp.concatenate([term, folded], axis=0).astype(BF16)
        out = dot(far_ref[...], dmean_ref[...])
        far_part_ref[...] = out.astype(BF16)


def layer(tiles, part, block, back, own, w_self, w_neigh, bias, cotangent, copies):
    rows, width = own.shape
    hid = w_self.shape[1]
    chunk_rows = 2 * width * hid // (copies * LANES)
    bias_rows = -(-hid // (LANES * SUBLANES)) * SUBLANES

    def tiled(columns):
        return pl.BlockSpec((NODE_TILE, columns), lambda i: (i, 0))

    outs = (
        jax.ShapeDtypeStruct((rows, hid), BF16),
        jax.ShapeDtypeStruct((copies, chunk_rows + bias_rows, LANES), BF16),
        jax.ShapeDtypeStruct((rows, width), F32),
        jax.ShapeDtypeStruct((rows, width), BF16),
        jax.ShapeDtypeStruct(((STEPS + 1 - CLOSE) * rows, width), BF16),
    )
    return pl.pallas_call(
        functools.partial(layer_kernel, back, chunk_rows),
        grid=(rows // NODE_TILE,),
        in_specs=[in_vmem()] * 7 + [tiled(width), tiled(hid)],
        out_specs=[tiled(hid)] + [whole(o) for o in outs[1:]],
        out_shape=outs,
        scratch_shapes=[
            pltpu.VMEM((width, rows), F32),
            pltpu.VMEM((2 * width, hid), F32),
            pltpu.VMEM((1, hid), F32),
            pltpu.VMEM((2 * width, hid), BF16),
        ],
        cost_estimate=pl.CostEstimate(
            flops=6 * rows * rows * width + 12 * rows * width * hid,
            bytes_accessed=4 * rows * hid,
            transcendentals=2 * rows * hid,
        ),
        compiler_params=pltpu.CompilerParams(vmem_limit_bytes=VMEM),
        name="layer",
    )(*tiles, part, block, w_self, w_neigh, bias, own, cotangent)


def spread_kernel(close_ref, dmean_ref, dself_ref, own_ref, near_ref):
    rows = dmean_ref.shape[0]
    dmean = dmean_ref[...]
    own_ref[...] = dself_ref[...] + dot(close_ref[:rows, :], dmean)
    near_ref[...] = dot(close_ref[rows:, :], dmean).astype(BF16)


def spread(tiles, dmean, dself):
    rows, width = dmean.shape
    return pl.pallas_call(
        spread_kernel,
        in_specs=[in_vmem()] * 3,
        out_specs=[in_vmem()] * 2,
        out_shape=(
            jax.ShapeDtypeStruct((rows, width), F32),
            jax.ShapeDtypeStruct(((CLOSE - 1) * rows, width), BF16),
        ),
        cost_estimate=pl.CostEstimate(
            flops=2 * CLOSE * rows * rows * width,
            bytes_accessed=2 * CLOSE * rows * width,
            transcendentals=0,
        ),
        compiler_params=pltpu.CompilerParams(vmem_limit_bytes=VMEM),
        name="spread",
    )(tiles[0], dmean, dself)


def unfold_kernel(chunks_ref, *out_refs):
    rows, columns = out_refs[0].shape
    copies, chunk_rows, lanes = chunks_ref.shape
    pieces = columns // lanes
    for chunk in range(copies):
        top, left = chunk // pieces * chunk_rows, chunk % pieces * lanes
        out_ref, top = out_refs[top // rows], top % rows
        out_ref[top : top + chunk_rows, left : left + lanes] = chunks_ref[chunk].astype(F32)


def unfold(chunks, rows, columns):
    return pl.pallas_call(
        unfold_kernel,
        out_shape=[jax.ShapeDtypeStruct((rows, columns), F32)] * 2,
        compiler_params=pltpu.CompilerParams(vmem_limit_bytes=VMEM),
        name="unfold",
    )(chunks)


def shift_pairs(by):
    sizes = [n for _, n in GRID]
    group = sizes[3] * sizes[4]
    peers = sizes[0] * sizes[1] * sizes[2]
    return [
        (b * group + r, ((b + by) % peers) * group + r) for b in range(peers) for r in range(group)
    ]


def shifted(array, by):
    return lax.ppermute(array, AXES, shift_pairs(by))


def exchange(array, axes):
    return lax.all_to_all(array, axes, 0, 0, tiled=True)


def sum_parts(array):
    return jnp.sum(array.astype(F32), axis=0)


def to_all(array, axes):
    return exchange(jnp.broadcast_to(array[None], (lax.axis_size(axes),) + array.shape), axes)


def shards(features, neighbours, w_self, w_neigh, bias, cotangent):
    rows, width = features.shape
    hid = w_self.shape[1]
    n_first = lax.axis_size(FIRST)
    near1 = shifted(features, 1)
    near2 = shifted(features, 2)
    near4 = shifted(features, 4)
    entries = neighbours.T
    tiles = count_tiles(entries, 0, CLOSE)
    near1, tiles, entries = lax.optimization_barrier((near1, tiles, entries))
    tiles = (tiles, count_tiles(entries, CLOSE, STEPS + 1 - CLOSE))
    near3 = shifted(near1, 2)
    part = gather_sum(tiles, (0, 2, 4, 1), (features, near2, near4, near1))
    hidden, send, dself, dmean, far = layer(
        tiles, part, near3, 3, features, w_self, w_neigh, bias[None], cotangent, n_first
    )
    far = shifted(far, -2)
    own, near = spread(tiles, dmean, dself)
    chunk = sum_parts(exchange(send, FIRST)).astype(BF16)
    far, _ = lax.optimization_barrier((far, chunk))
    near = near.astype(F32) + far.astype(F32)
    got1 = shifted(near[:rows].astype(BF16), -1)
    got2 = shifted(near[rows:].astype(BF16), -2)

    scale = 1.0 / (rows * lax.axis_size(AXES)) ** 0.5
    total = sum_parts(to_all(chunk, SECOND)) * scale
    pieces = hid // LANES
    chunk_rows = 2 * width * pieces // n_first
    grads = unfold(to_all(total[:chunk_rows].astype(BF16), FIRST), width, hid)
    g_bias = total[chunk_rows : chunk_rows + pieces].reshape(hid)
    grad_x = own + got1.astype(F32) + got2.astype(F32)
    return hidden, grad_x.astype(BF16), *grads, g_bias


def solution(mesh):
    grid = Mesh(mesh.devices.reshape([n for _, n in GRID]), AXES)
    node = P(AXES, None)
    return jax.shard_map(
        shards,
        mesh=grid,
        in_specs=(node, node, P(), P(), P(), node),
        out_specs=(node, node, P(), P(), P()),
        check_vma=False,
    )
```

```python
import functools

import jax
import jax.numpy as jnp
import numpy as np
from jax import lax
from jax.experimental import pallas as pl
from jax.experimental.pallas import tpu as pltpu
from jax.sharding import Mesh
from jax.sharding import PartitionSpec as P

FAN = 10
STEPS = 4
CLOSE = 3
WINDOW_TILE = 256
NODE_TILE = 256
LANES = 128
SUBLANES = 8
PACK = 16
VMEM = 24 * 1024 * 1024
BF16 = jnp.bfloat16
F32 = jnp.float32

GRID = (("x", 4), ("z", 12), ("far", 2), ("near", 4), ("core", 2))
AXES = tuple(name for name, _ in GRID)
FIRST = ("x", "far", "near", "core")
SECOND = ("z",)

ROWS_FIRST = (((0,), (0,)), ((), ()))
COLS_LAST = (((1,), (1,)), ((), ()))


def dot(a, b, contract=(((1,), (0,)), ((), ()))):
    return lax.dot_general(a, b, contract, preferred_element_type=F32)


def count_kernel(first, near_ref, out_ref):
    row = lax.broadcasted_iota(jnp.int32, (PACK, LANES), 0)
    rows = [(row + PACK * g).astype(jnp.int16) for g in range(WINDOW_TILE // PACK)]
    one = jnp.ones((PACK, LANES), BF16)
    zero = jnp.zeros((PACK, LANES), BF16)

    @pl.loop(0, out_ref.shape[0] // WINDOW_TILE)
    def _(step):
        low = pl.multiple_of(step * WINDOW_TILE, WINDOW_TILE)
        key = (near_ref[...] - (first + low)).astype(jnp.int16)
        for lane in range(near_ref.shape[1] // LANES):
            cols = slice(lane * LANES, (lane + 1) * LANES)
            keys = [jnp.broadcast_to(key[k : k + 1, cols], (PACK, LANES)) for k in range(FAN)]
            for g in range(WINDOW_TILE // PACK):
                count = jnp.where(rows[g] == keys[0], one, zero)
                for k in range(1, FAN):
                    count = count + jnp.where(rows[g] == keys[k], one, zero)
                out_ref[pl.ds(low + g * PACK, PACK), cols] = count


def in_vmem():
    return pl.BlockSpec(memory_space=pltpu.VMEM)


def count_tiles(near, first, blocks):
    entries, rows = near.shape
    window = blocks * rows
    return pl.pallas_call(
        functools.partial(count_kernel, first * rows),
        in_specs=[in_vmem()],
        out_specs=in_vmem(),
        out_shape=jax.ShapeDtypeStruct((window, rows), BF16),
        cost_estimate=pl.CostEstimate(
            flops=3 * entries * window * rows, bytes_accessed=2 * window * rows, transcendentals=0
        ),
        compiler_params=pltpu.CompilerParams(vmem_limit_bytes=VMEM),
        name="count_tiles",
    )(near)


def whole(array):
    return pl.BlockSpec(array.shape, lambda *_: (0,) * array.ndim)


def tile_of(back, close_ref, far_ref):
    rows = close_ref.shape[1]
    ref, first = (close_ref, 0) if back < CLOSE else (far_ref, CLOSE)
    return ref[(back - first) * rows : (back - first + 1) * rows, :]


def gather_kernel(window_blocks, close_ref, far_ref, *refs):
    *blocks, out_ref = refs
    total = None
    for back, block in zip(window_blocks, blocks):
        term = dot(block[...], tile_of(back, close_ref, far_ref), ROWS_FIRST)
        total = term if total is None else total + term
    out_ref[...] = total


def gather_sum(tiles, window_blocks, blocks):
    rows, width = blocks[0].shape
    steps = len(blocks)
    return pl.pallas_call(
        functools.partial(gather_kernel, window_blocks),
        in_specs=[in_vmem()] * (2 + steps),
        out_specs=in_vmem(),
        out_shape=jax.ShapeDtypeStruct((width, rows), F32),
        cost_estimate=pl.CostEstimate(
            flops=2 * steps * rows * rows * width,
            bytes_accessed=2 * steps * rows * width,
            transcendentals=0,
        ),
        compiler_params=pltpu.CompilerParams(vmem_limit_bytes=VMEM),
        name="gather_sum",
    )(*tiles, *blocks)


def layer_kernel(
    back,
    chunk_rows,
    close_ref,
    far_ref,
    part_ref,
    block_ref,
    w_self_ref,
    w_neigh_ref,
    bias_ref,
    own_ref,
    cot_ref,
    hidden_ref,
    send_ref,
    dself_ref,
    dmean_ref,
    far_part_ref,
    total_ref,
    grad_ref,
    gbias_ref,
    w_ref,
):
    rows, width = block_ref.shape
    hid = w_ref.shape[1]
    step = pl.program_id(0)

    @pl.when(step == 0)
    def _():
        tile = tile_of(back, close_ref, far_ref)
        total_ref[...] = part_ref[...] + dot(block_ref[...], tile, ROWS_FIRST)
        grad_ref[...] = jnp.zeros_like(grad_ref)
        gbias_ref[...] = jnp.zeros_like(gbias_ref)
        w_ref[:width, :] = w_self_ref[...]
        w_ref[width:, :] = w_neigh_ref[...]

    weights = w_ref[...]
    span = pl.ds(pl.multiple_of(step * NODE_TILE, NODE_TILE), NODE_TILE)
    mean = (total_ref[:, span].T / FAN).astype(BF16)
    both = jnp.concatenate([own_ref[...], mean], axis=1)
    pre = dot(both, weights) + bias_ref[...]
    sig = jax.nn.sigmoid(pre)
    hidden_ref[...] = (pre * sig).astype(BF16)
    slope = sig * (1.0 + pre * (1.0 - sig))
    dpre = (cot_ref[...].astype(F32) * slope).astype(BF16)
    grad_ref[...] += dot(both, dpre, ROWS_FIRST)
    gbias_ref[...] += jnp.sum(dpre.astype(F32), axis=0, keepdims=True)
    back_both = dot(dpre, weights, COLS_LAST)
    dself_ref[span, :] = back_both[:, :width]
    dmean_ref[span, :] = (back_both[:, width:] / FAN).astype(BF16)

    @pl.when(step == pl.num_programs(0) - 1)
    def _():
        pieces = hid // LANES
        spare = send_ref.shape[1] - chunk_rows - pieces
        folded = [gbias_ref[:, p * LANES : (p + 1) * LANES] for p in range(pieces)]
        folded = jnp.concatenate([*folded, jnp.zeros((spare, LANES), F32)], axis=0)
        for chunk in range(send_ref.shape[0]):
            top, left = chunk // pieces * chunk_rows, chunk % pieces * LANES
            term = grad_ref[top : top + chunk_rows, left : left + LANES]
            send_ref[chunk] = jnp.concatenate([term, folded], axis=0).astype(BF16)
        out = dot(far_ref[...], dmean_ref[...])
        far_part_ref[...] = out.astype(BF16)


def layer(tiles, part, block, back, own, w_self, w_neigh, bias, cotangent, copies):
    rows, width = own.shape
    hid = w_self.shape[1]
    chunk_rows = 2 * width * hid // (copies * LANES)
    bias_rows = -(-hid // (LANES * SUBLANES)) * SUBLANES

    def tiled(columns):
        return pl.BlockSpec((NODE_TILE, columns), lambda i: (i, 0))

    outs = (
        jax.ShapeDtypeStruct((rows, hid), BF16),
        jax.ShapeDtypeStruct((copies, chunk_rows + bias_rows, LANES), BF16),
        jax.ShapeDtypeStruct((rows, width), F32),
        jax.ShapeDtypeStruct((rows, width), BF16),
        jax.ShapeDtypeStruct(((STEPS + 1 - CLOSE) * rows, width), BF16),
    )
    return pl.pallas_call(
        functools.partial(layer_kernel, back, chunk_rows),
        grid=(rows // NODE_TILE,),
        in_specs=[in_vmem()] * 7 + [tiled(width), tiled(hid)],
        out_specs=[tiled(hid)] + [whole(o) for o in outs[1:]],
        out_shape=outs,
        scratch_shapes=[
            pltpu.VMEM((width, rows), F32),
            pltpu.VMEM((2 * width, hid), F32),
            pltpu.VMEM((1, hid), F32),
            pltpu.VMEM((2 * width, hid), BF16),
        ],
        cost_estimate=pl.CostEstimate(
            flops=6 * rows * rows * width + 12 * rows * width * hid,
            bytes_accessed=4 * rows * hid,
            transcendentals=2 * rows * hid,
        ),
        compiler_params=pltpu.CompilerParams(vmem_limit_bytes=VMEM),
        name="layer",
    )(*tiles, part, block, w_self, w_neigh, bias, own, cotangent)


def spread_kernel(close_ref, dmean_ref, dself_ref, own_ref, near_ref):
    rows = dmean_ref.shape[0]
    dmean = dmean_ref[...]
    own_ref[...] = dself_ref[...] + dot(close_ref[:rows, :], dmean)
    near_ref[...] = dot(close_ref[rows:, :], dmean).astype(BF16)


def spread(tiles, dmean, dself):
    rows, width = dmean.shape
    return pl.pallas_call(
        spread_kernel,
        in_specs=[in_vmem()] * 3,
        out_specs=[in_vmem()] * 2,
        out_shape=(
            jax.ShapeDtypeStruct((rows, width), F32),
            jax.ShapeDtypeStruct(((CLOSE - 1) * rows, width), BF16),
        ),
        cost_estimate=pl.CostEstimate(
            flops=2 * CLOSE * rows * rows * width,
            bytes_accessed=2 * CLOSE * rows * width,
            transcendentals=0,
        ),
        compiler_params=pltpu.CompilerParams(vmem_limit_bytes=VMEM),
        name="spread",
    )(tiles[0], dmean, dself)


def unfold_kernel(chunks_ref, *out_refs):
    rows, columns = out_refs[0].shape
    copies, chunk_rows, lanes = chunks_ref.shape
    pieces = columns // lanes
    for chunk in range(copies):
        top, left = chunk // pieces * chunk_rows, chunk % pieces * lanes
        out_ref, top = out_refs[top // rows], top % rows
        out_ref[top : top + chunk_rows, left : left + lanes] = chunks_ref[chunk].astype(F32)


def unfold(chunks, rows, columns):
    return pl.pallas_call(
        unfold_kernel,
        out_shape=[jax.ShapeDtypeStruct((rows, columns), F32)] * 2,
        compiler_params=pltpu.CompilerParams(vmem_limit_bytes=VMEM),
        name="unfold",
    )(chunks)


def shift_pairs(by):
    sizes = [n for _, n in GRID]
    group = sizes[3] * sizes[4]
    peers = sizes[0] * sizes[1] * sizes[2]
    return [
        (b * group + r, ((b + by) % peers) * group + r) for b in range(peers) for r in range(group)
    ]


def shifted(array, by):
    return lax.ppermute(array, AXES, shift_pairs(by))


def exchange(array, axes):
    return lax.all_to_all(array, axes, 0, 0, tiled=True)


def sum_parts(array):
    return jnp.sum(array.astype(F32), axis=0)


def to_all(array, axes):
    return exchange(jnp.broadcast_to(array[None], (lax.axis_size(axes),) + array.shape), axes)


def shards(features, neighbours, w_self, w_neigh, bias, cotangent):
    rows, width = features.shape
    hid = w_self.shape[1]
    n_first = lax.axis_size(FIRST)
    near1 = shifted(features, 1)
    near2 = shifted(features, 2)
    entries = neighbours.T
    tiles = count_tiles(entries, 0, CLOSE)
    near2, tiles = lax.optimization_barrier((near2, tiles))
    near4 = shifted(near2, 2)
    near1, tiles, entries = lax.optimization_barrier((near1, tiles, entries))
    tiles = (tiles, count_tiles(entries, CLOSE, STEPS + 1 - CLOSE))
    near3 = shifted(near1, 2)
    part = gather_sum(tiles, (0, 2, 4, 1), (features, near2, near4, near1))
    hidden, send, dself, dmean, far = layer(
        tiles, part, near3, 3, features, w_self, w_neigh, bias[None], cotangent, n_first
    )
    far = shifted(far, -2)
    own, near = spread(tiles, dmean, dself)
    chunk = sum_parts(exchange(send, FIRST)).astype(BF16)
    far, _ = lax.optimization_barrier((far, chunk))
    near = near.astype(F32) + far.astype(F32)
    got1 = shifted(near[:rows].astype(BF16), -1)
    got2 = shifted(near[rows:].astype(BF16), -2)

    scale = 1.0 / (rows * lax.axis_size(AXES)) ** 0.5
    total = sum_parts(to_all(chunk, SECOND)) * scale
    pieces = hid // LANES
    chunk_rows = 2 * width * pieces // n_first
    grads = unfold(to_all(total[:chunk_rows].astype(BF16), FIRST), width, hid)
    g_bias = total[chunk_rows : chunk_rows + pieces].reshape(hid)
    grad_x = own + got1.astype(F32) + got2.astype(F32)
    return hidden, grad_x.astype(BF16), *grads, g_bias


def solution(mesh):
    grid = Mesh(mesh.devices.reshape([n for _, n in GRID]), AXES)
    node = P(AXES, None)
    return jax.shard_map(
        shards,
        mesh=grid,
        in_specs=(node, node, P(), P(), P(), node),
        out_specs=(node, node, P(), P(), P()),
        check_vma=False,
    )
```

```python
import functools

import jax
import jax.numpy as jnp
import numpy as np
from jax import lax
from jax.experimental import pallas as pl
from jax.experimental.pallas import tpu as pltpu
from jax.sharding import Mesh
from jax.sharding import PartitionSpec as P

FAN = 10
STEPS = 4
CLOSE = 3
WINDOW_TILE = 256
NODE_TILE = 512
LANES = 128
SUBLANES = 8
PACK = 16
VMEM = 24 * 1024 * 1024
BF16 = jnp.bfloat16
F32 = jnp.float32

GRID = (("x", 4), ("z", 12), ("far", 2), ("near", 4), ("core", 2))
AXES = tuple(name for name, _ in GRID)
FIRST = ("x", "far", "near", "core")
SECOND = ("z",)

ROWS_FIRST = (((0,), (0,)), ((), ()))
COLS_LAST = (((1,), (1,)), ((), ()))


def dot(a, b, contract=(((1,), (0,)), ((), ()))):
    return lax.dot_general(a, b, contract, preferred_element_type=F32)


def count_kernel(first, near_ref, out_ref):
    row = lax.broadcasted_iota(jnp.int32, (PACK, LANES), 0)
    rows = [(row + PACK * g).astype(jnp.int16) for g in range(WINDOW_TILE // PACK)]
    one = jnp.ones((PACK, LANES), BF16)
    zero = jnp.zeros((PACK, LANES), BF16)

    @pl.loop(0, out_ref.shape[0] // WINDOW_TILE)
    def _(step):
        low = pl.multiple_of(step * WINDOW_TILE, WINDOW_TILE)
        key = (near_ref[...] - (first + low)).astype(jnp.int16)
        for lane in range(near_ref.shape[1] // LANES):
            cols = slice(lane * LANES, (lane + 1) * LANES)
            keys = [jnp.broadcast_to(key[k : k + 1, cols], (PACK, LANES)) for k in range(FAN)]
            for g in range(WINDOW_TILE // PACK):
                count = jnp.where(rows[g] == keys[0], one, zero)
                for k in range(1, FAN):
                    count = count + jnp.where(rows[g] == keys[k], one, zero)
                out_ref[pl.ds(low + g * PACK, PACK), cols] = count


def in_vmem():
    return pl.BlockSpec(memory_space=pltpu.VMEM)


def count_tiles(near, first, blocks):
    entries, rows = near.shape
    window = blocks * rows
    return pl.pallas_call(
        functools.partial(count_kernel, first * rows),
        in_specs=[in_vmem()],
        out_specs=in_vmem(),
        out_shape=jax.ShapeDtypeStruct((window, rows), BF16),
        cost_estimate=pl.CostEstimate(
            flops=3 * entries * window * rows, bytes_accessed=2 * window * rows, transcendentals=0
        ),
        compiler_params=pltpu.CompilerParams(vmem_limit_bytes=VMEM),
        name="count_tiles",
    )(near)


def whole(array):
    return pl.BlockSpec(array.shape, lambda *_: (0,) * array.ndim)


def tile_of(back, close_ref, far_ref):
    rows = close_ref.shape[1]
    ref, first = (close_ref, 0) if back < CLOSE else (far_ref, CLOSE)
    return ref[(back - first) * rows : (back - first + 1) * rows, :]


def gather_kernel(window_blocks, close_ref, far_ref, *refs):
    *blocks, out_ref = refs
    total = None
    for back, block in zip(window_blocks, blocks):
        term = dot(block[...], tile_of(back, close_ref, far_ref), ROWS_FIRST)
        total = term if total is None else total + term
    out_ref[...] = total


def gather_sum(tiles, window_blocks, blocks):
    rows, width = blocks[0].shape
    steps = len(blocks)
    return pl.pallas_call(
        functools.partial(gather_kernel, window_blocks),
        in_specs=[in_vmem()] * (2 + steps),
        out_specs=in_vmem(),
        out_shape=jax.ShapeDtypeStruct((width, rows), F32),
        cost_estimate=pl.CostEstimate(
            flops=2 * steps * rows * rows * width,
            bytes_accessed=2 * steps * rows * width,
            transcendentals=0,
        ),
        compiler_params=pltpu.CompilerParams(vmem_limit_bytes=VMEM),
        name="gather_sum",
    )(*tiles, *blocks)


def layer_kernel(
    back,
    chunk_rows,
    close_ref,
    far_ref,
    part_ref,
    block_ref,
    w_self_ref,
    w_neigh_ref,
    bias_ref,
    own_ref,
    cot_ref,
    hidden_ref,
    send_ref,
    dself_ref,
    dmean_ref,
    far_part_ref,
    total_ref,
    grad_ref,
    gbias_ref,
    w_ref,
):
    rows, width = block_ref.shape
    hid = w_ref.shape[1]
    step = pl.program_id(0)

    @pl.when(step == 0)
    def _():
        tile = tile_of(back, close_ref, far_ref)
        total_ref[...] = part_ref[...] + dot(block_ref[...], tile, ROWS_FIRST)
        grad_ref[...] = jnp.zeros_like(grad_ref)
        gbias_ref[...] = jnp.zeros_like(gbias_ref)
        w_ref[:width, :] = w_self_ref[...]
        w_ref[width:, :] = w_neigh_ref[...]

    weights = w_ref[...]
    span = pl.ds(pl.multiple_of(step * NODE_TILE, NODE_TILE), NODE_TILE)
    mean = (total_ref[:, span].T / FAN).astype(BF16)
    both = jnp.concatenate([own_ref[...], mean], axis=1)
    pre = dot(both, weights) + bias_ref[...]
    sig = jax.nn.sigmoid(pre)
    hidden_ref[...] = (pre * sig).astype(BF16)
    slope = sig * (1.0 + pre * (1.0 - sig))
    dpre = (cot_ref[...].astype(F32) * slope).astype(BF16)
    grad_ref[...] += dot(both, dpre, ROWS_FIRST)
    gbias_ref[...] += jnp.sum(dpre.astype(F32), axis=0, keepdims=True)
    back_both = dot(dpre, weights, COLS_LAST)
    dself_ref[span, :] = back_both[:, :width]
    dmean_ref[span, :] = (back_both[:, width:] / FAN).astype(BF16)

    @pl.when(step == pl.num_programs(0) - 1)
    def _():
        pieces = hid // LANES
        spare = send_ref.shape[1] - chunk_rows - pieces
        folded = [gbias_ref[:, p * LANES : (p + 1) * LANES] for p in range(pieces)]
        folded = jnp.concatenate([*folded, jnp.zeros((spare, LANES), F32)], axis=0)
        for chunk in range(send_ref.shape[0]):
            top, left = chunk // pieces * chunk_rows, chunk % pieces * LANES
            term = grad_ref[top : top + chunk_rows, left : left + LANES]
            send_ref[chunk] = jnp.concatenate([term, folded], axis=0).astype(BF16)
        out = dot(far_ref[...], dmean_ref[...])
        far_part_ref[...] = out.astype(BF16)


def layer(tiles, part, block, back, own, w_self, w_neigh, bias, cotangent, copies):
    rows, width = own.shape
    hid = w_self.shape[1]
    chunk_rows = 2 * width * hid // (copies * LANES)
    bias_rows = -(-hid // (LANES * SUBLANES)) * SUBLANES

    def tiled(columns):
        return pl.BlockSpec((NODE_TILE, columns), lambda i: (i, 0))

    outs = (
        jax.ShapeDtypeStruct((rows, hid), BF16),
        jax.ShapeDtypeStruct((copies, chunk_rows + bias_rows, LANES), BF16),
        jax.ShapeDtypeStruct((rows, width), F32),
        jax.ShapeDtypeStruct((rows, width), BF16),
        jax.ShapeDtypeStruct(((STEPS + 1 - CLOSE) * rows, width), BF16),
    )
    return pl.pallas_call(
        functools.partial(layer_kernel, back, chunk_rows),
        grid=(rows // NODE_TILE,),
        in_specs=[in_vmem()] * 7 + [tiled(width), tiled(hid)],
        out_specs=[tiled(hid)] + [whole(o) for o in outs[1:]],
        out_shape=outs,
        scratch_shapes=[
            pltpu.VMEM((width, rows), F32),
            pltpu.VMEM((2 * width, hid), F32),
            pltpu.VMEM((1, hid), F32),
            pltpu.VMEM((2 * width, hid), BF16),
        ],
        cost_estimate=pl.CostEstimate(
            flops=6 * rows * rows * width + 12 * rows * width * hid,
            bytes_accessed=4 * rows * hid,
            transcendentals=2 * rows * hid,
        ),
        compiler_params=pltpu.CompilerParams(vmem_limit_bytes=VMEM),
        name="layer",
    )(*tiles, part, block, w_self, w_neigh, bias, own, cotangent)


def spread_kernel(close_ref, dmean_ref, dself_ref, own_ref, near_ref):
    rows = dmean_ref.shape[0]
    dmean = dmean_ref[...]
    own_ref[...] = dself_ref[...] + dot(close_ref[:rows, :], dmean)
    near_ref[...] = dot(close_ref[rows:, :], dmean).astype(BF16)


def spread(tiles, dmean, dself):
    rows, width = dmean.shape
    return pl.pallas_call(
        spread_kernel,
        in_specs=[in_vmem()] * 3,
        out_specs=[in_vmem()] * 2,
        out_shape=(
            jax.ShapeDtypeStruct((rows, width), F32),
            jax.ShapeDtypeStruct(((CLOSE - 1) * rows, width), BF16),
        ),
        cost_estimate=pl.CostEstimate(
            flops=2 * CLOSE * rows * rows * width,
            bytes_accessed=2 * CLOSE * rows * width,
            transcendentals=0,
        ),
        compiler_params=pltpu.CompilerParams(vmem_limit_bytes=VMEM),
        name="spread",
    )(tiles[0], dmean, dself)


def unfold_kernel(chunks_ref, *out_refs):
    rows, columns = out_refs[0].shape
    copies, chunk_rows, lanes = chunks_ref.shape
    pieces = columns // lanes
    for chunk in range(copies):
        top, left = chunk // pieces * chunk_rows, chunk % pieces * lanes
        out_ref, top = out_refs[top // rows], top % rows
        out_ref[top : top + chunk_rows, left : left + lanes] = chunks_ref[chunk].astype(F32)


def unfold(chunks, rows, columns):
    return pl.pallas_call(
        unfold_kernel,
        out_shape=[jax.ShapeDtypeStruct((rows, columns), F32)] * 2,
        compiler_params=pltpu.CompilerParams(vmem_limit_bytes=VMEM),
        name="unfold",
    )(chunks)


def shift_pairs(by):
    sizes = [n for _, n in GRID]
    group = sizes[3] * sizes[4]
    peers = sizes[0] * sizes[1] * sizes[2]
    return [
        (b * group + r, ((b + by) % peers) * group + r) for b in range(peers) for r in range(group)
    ]


def shifted(array, by):
    return lax.ppermute(array, AXES, shift_pairs(by))


def exchange(array, axes):
    return lax.all_to_all(array, axes, 0, 0, tiled=True)


def sum_parts(array):
    return jnp.sum(array.astype(F32), axis=0)


def to_all(array, axes):
    return exchange(jnp.broadcast_to(array[None], (lax.axis_size(axes),) + array.shape), axes)


def shards(features, neighbours, w_self, w_neigh, bias, cotangent):
    rows, width = features.shape
    hid = w_self.shape[1]
    n_first = lax.axis_size(FIRST)
    near1 = shifted(features, 1)
    near2 = shifted(features, 2)
    entries = neighbours.T
    tiles = count_tiles(entries, 0, CLOSE)
    near2, tiles = lax.optimization_barrier((near2, tiles))
    near4 = shifted(near2, 2)
    near1, tiles, entries = lax.optimization_barrier((near1, tiles, entries))
    tiles = (tiles, count_tiles(entries, CLOSE, STEPS + 1 - CLOSE))
    near3 = shifted(near1, 2)
    part = gather_sum(tiles, (0, 2, 4, 1), (features, near2, near4, near1))
    hidden, send, dself, dmean, far = layer(
        tiles, part, near3, 3, features, w_self, w_neigh, bias[None], cotangent, n_first
    )
    far = shifted(far, -2)
    own, near = spread(tiles, dmean, dself)
    chunk = sum_parts(exchange(send, FIRST)).astype(BF16)
    far, _ = lax.optimization_barrier((far, chunk))
    near = near.astype(F32) + far.astype(F32)
    got1 = shifted(near[:rows].astype(BF16), -1)
    got2 = shifted(near[rows:].astype(BF16), -2)

    scale = 1.0 / (rows * lax.axis_size(AXES)) ** 0.5
    total = sum_parts(to_all(chunk, SECOND)) * scale
    pieces = hid // LANES
    chunk_rows = 2 * width * pieces // n_first
    grads = unfold(to_all(total[:chunk_rows].astype(BF16), FIRST), width, hid)
    g_bias = total[chunk_rows : chunk_rows + pieces].reshape(hid)
    grad_x = own + got1.astype(F32) + got2.astype(F32)
    return hidden, grad_x.astype(BF16), *grads, g_bias


def solution(mesh):
    grid = Mesh(mesh.devices.reshape([n for _, n in GRID]), AXES)
    node = P(AXES, None)
    return jax.shard_map(
        shards,
        mesh=grid,
        in_specs=(node, node, P(), P(), P(), node),
        out_specs=(node, node, P(), P(), P()),
        check_vma=False,
    )
```
